32 devices in a mesh: req: 4 (over x, core), seq: 8 (over z, y).
Axes of the slice: x: 2, y: 2, z: 4, core: 2. Of those that a mesh axis runs over, the one named last changes fastest.
Arguments:
- hidden: bfloat16 [4, 1024, 2048], P('req', 'seq'), may hold values from -6 to 6
- lengths: int32 [4], replicated, may hold values from 1 to 1024, 2560 in all
- slot_request: int32 [4], replicated, may hold values from 0 to 3, each once
- norm_gain: bfloat16 [2048], replicated, may hold values from 0.099609375 to 1.8984375
- in_weight: bfloat16 [2, 2048, 4096], P(None, 'req', 'seq'), may hold values from -0.125 to 0.125
- conv_weight: bfloat16 [4, 4096], P(None, 'seq'), may hold values from -3 to 3
- conv_bias: bfloat16 [4096], P('seq'), may hold values from -0.5 to 0.5
- xproj_weight: bfloat16 [4096, 160], P('seq'), may hold values from -0.09375 to 0.09375
- dt_weight: bfloat16 [128, 4096], P(None, 'seq'), may hold values from -0.5 to 0.5
- dt_bias: bfloat16 [4096], P('seq'), may hold values from -6.91 to -2.25
- a_log: float32 [16, 4096], replicated, may hold values from -2.3 to 1.39
- skip_gain: float32 [4096], replicated, may hold values from 0.5 to 1.5
- out_weight: bfloat16 [4096, 2048], P('seq', 'req'), may hold values from -0.09375 to 0.09375
Outputs:
- mixed: bfloat16 [4, 1024, 2048], P('req', 'seq')
- final_state: float32 [4, 16, 4096], P('req', None, 'seq')
The draws below stay inside these ranges and needn't reach their ends.
Inputs may be any that keep to these rules, and one draw needn't show every extreme that they name: `lengths`: each slot's length is at least 1, the longest is exactly 1024, and they sum to 2560. `slot_request`: A permutation of the requests.
All inputs are finite; a program needn't handle non-finite values.
Results may differ from the reference program's by a relative error of at most 0.015.
Values may be sent and summed in bfloat16 or wider, within the bound.
A program may use at most 128 MiB of HBM per device.

```python
import math
import jax
import jax.numpy as jnp
import numpy as np
from jax import lax

D = 2048
INNER = 4096
STATE = 16
RANK = 128
CONV = 4
LEN = 1024
REQS = 4


def draw_dt_bias(key, part):
    first, second, third = jax.random.split(key, 3)
    share = 0.5
    slow = jax.random.uniform(first, (INNER,), jnp.float32) < share
    slow_rate = jnp.exp(jax.random.uniform(second, (INNER,), jnp.float32, math.log(0.001), math.log(0.005)))
    fast_rate = jnp.exp(jax.random.uniform(third, (INNER,), jnp.float32, math.log(0.01), math.log(0.1)))
    rate = jnp.where(slow, slow_rate, fast_rate)
    return jnp.log(jnp.expm1(rate)).astype(jnp.bfloat16)


def block_scale(own_key, extent, shards, low, high):
    gain = 1.0
    for dim, parts in shards:
        steps = jax.random.uniform(jax.random.fold_in(jax.random.fold_in(own_key, 6), dim), (parts,), jnp.float32, low / len(shards), high / len(shards))
        gain = gain * jnp.repeat(jnp.exp(steps), extent[dim] // parts).reshape((-1,) + (1,) * (len(extent) - 1 - dim))
    return gain


def split_up(count, total, limit, skew):
    portions = [(1 << 20) // math.isqrt(grade ** skew) + 1 for grade in range(2, count + 1)]
    surplus, holding = total - limit - (count - 1), [1] * (count - 1)
    while surplus > 0:
        movable = [i for i in range(count - 1) if holding[i] < limit]
        whole, remaining = sum([portions[i] for i in movable]), surplus
        for i in movable:
            addition = min(limit - holding[i], max(1, remaining * portions[i] // whole), surplus)
            holding[i] = holding[i] + addition
            surplus = surplus - addition
    return np.array([limit] + holding)


def ragged(rng, count, total, reach, slope):
    if count == 2:
        one = jax.random.randint(rng, (), max(1, total - reach), min(reach, total - 1) + 1)
        return jnp.stack([one, total - one])
    tallies = jnp.asarray(split_up(count, total, reach, slope), jnp.int32)
    pairs = (count - 1) // 2
    giver, sink = tallies[1:1 + 2 * pairs:2], tallies[2:2 + 2 * pairs:2]
    margin = jnp.minimum(giver - 1, reach - sink)
    shifted = jax.random.randint(jax.random.fold_in(rng, 1), (pairs,), 0, 1 << 20) % (margin + 1)
    tallies = tallies.at[1:1 + 2 * pairs:2].set(giver - shifted).at[2:2 + 2 * pairs:2].set(sink + shifted)
    return tallies[jax.random.permutation(jax.random.fold_in(rng, 2), count)]


def bell_draw(key, dims, spread, bound, pieces=(), kind=jnp.bfloat16):
    loudness = block_scale(key, dims, pieces, -0.22, 0.18) if pieces else 1.0
    drawn = jax.random.normal(key, dims, jnp.float32) * spread * loudness
    return jnp.minimum(jnp.maximum(drawn, -bound), bound).astype(kind)


def setup_inputs(seed: int = 0) -> dict:
    arg_keys = jax.random.split(jax.random.key(seed), 14)
    hidden = bell_draw(arg_keys[0], (REQS, LEN, D), 1.0, 6.0, ((0, 4), (1, 8)))
    lengths = ragged(arg_keys[1], REQS, 5 * REQS * LEN // 8, LEN, 2).astype(jnp.int32)
    slot_request = jax.random.permutation(arg_keys[2], REQS).astype(jnp.int32)
    norm_gain = jnp.clip(1.0 + 0.18 * jax.random.normal(arg_keys[3], (D,), jnp.float32), 0.099609375, 1.8984375).astype(jnp.bfloat16)
    in_weight = bell_draw(arg_keys[4], (2, D, INNER), D ** -0.5, 0.125, ((1, 4), (2, 8)))
    conv_weight = bell_draw(arg_keys[5], (CONV, INNER), CONV ** -0.5, 3.0, ((1, 8),))
    conv_bias = jnp.clip(jax.random.uniform(arg_keys[6], (INNER,), jnp.float32, -0.5, 0.5) * block_scale(arg_keys[6], (INNER,), ((0, 8),), -0.4, 0.0), -0.5, 0.5).astype(jnp.bfloat16)
    xproj_weight = bell_draw(arg_keys[7], (INNER, RANK + 2 * STATE), INNER ** -0.5, 0.09375, ((0, 8),))
    dt_weight = bell_draw(arg_keys[8], (RANK, INNER), RANK ** -0.5, 0.5, ((1, 8),))
    dt_bias = draw_dt_bias(jax.random.fold_in(arg_keys[13], 71), 0)
    a_log = jnp.clip(jax.random.uniform(arg_keys[10], (STATE, INNER), jnp.float32, -2.3, 1.39), -2.3, 1.39)
    skip_gain = jnp.clip(jax.random.uniform(arg_keys[11], (INNER,), jnp.float32, 0.5, 1.5), 0.5, 1.5)
    out_weight = bell_draw(arg_keys[12], (INNER, D), INNER ** -0.5, 0.09375, ((0, 8), (1, 4)))
    return {"hidden": hidden, "lengths": lengths, "slot_request": slot_request, "norm_gain": norm_gain, "in_weight": in_weight, "conv_weight": conv_weight, "conv_bias": conv_bias, "xproj_weight": xproj_weight, "dt_weight": dt_weight, "dt_bias": dt_bias, "a_log": a_log, "skip_gain": skip_gain, "out_weight": out_weight}


def reference(hidden, lengths, slot_request, norm_gain, in_weight, conv_weight, conv_bias, xproj_weight, dt_weight, dt_bias, a_log, skip_gain, out_weight):
    tokens = hidden.astype(jnp.float32)
    scale = lax.rsqrt(lax.optimization_barrier(jnp.mean(tokens * tokens, axis=-1, keepdims=True)) + 1e-05)
    normed = (tokens * scale * norm_gain.astype(jnp.float32)).astype(jnp.bfloat16)
    flat = normed.reshape(REQS * LEN, D)
    xin = jnp.dot(flat, in_weight[0], preferred_element_type=jnp.float32).reshape(REQS, LEN, INNER)
    zgate = jnp.dot(flat, in_weight[1], preferred_element_type=jnp.float32).astype(jnp.bfloat16).reshape(REQS, LEN, INNER)
    padded = jnp.pad(xin, ((0, 0), (CONV - 1, 0), (0, 0)))
    taps = conv_weight.astype(jnp.float32)
    convolved = conv_bias.astype(jnp.float32) + jnp.zeros_like(xin)
    for tap in range(CONV):
        convolved = convolved + taps[tap] * padded[:, tap:tap + LEN, :]
    inner = jax.nn.silu(convolved).astype(jnp.bfloat16)
    proj = jnp.dot(inner.reshape(REQS * LEN, INNER), xproj_weight, preferred_element_type=jnp.float32)
    rate_low = proj[:, :RANK].astype(jnp.bfloat16)
    entry = proj[:, RANK:RANK + STATE].reshape(REQS, LEN, STATE)
    readout = proj[:, RANK + STATE:].reshape(REQS, LEN, STATE)
    live = (jnp.arange(LEN, dtype=jnp.int32)[None, :] < lengths[:, None]).astype(jnp.float32)
    delta = jax.nn.softplus(jnp.dot(rate_low, dt_weight, preferred_element_type=jnp.float32) + dt_bias.astype(jnp.float32))
    delta = delta.reshape(REQS, LEN, INNER) * live[:, :, None]
    decay = -jnp.exp(a_log)
    inner_f = inner.astype(jnp.float32)

    def advance(state, items):
        rate, value, into, outof = items
        state = jnp.exp(rate[:, None, :] * decay[None]) * state + (rate * value)[:, None, :] * into[:, :, None]
        result = lax.optimization_barrier(jnp.sum(outof[:, :, None] * state, axis=1)) + skip_gain * value
        return (state, result)
    moved = (jnp.swapaxes(delta, 0, 1), jnp.swapaxes(inner_f, 0, 1), jnp.swapaxes(entry, 0, 1), jnp.swapaxes(readout, 0, 1))
    start = jnp.zeros((REQS, STATE, INNER), jnp.float32)
    last, results = lax.scan(advance, start, moved)
    scanned = jnp.swapaxes(results, 0, 1).astype(jnp.bfloat16)
    gated = (scanned.astype(jnp.float32) * jax.nn.silu(zgate.astype(jnp.float32))).astype(jnp.bfloat16)
    branch = jnp.dot(gated.reshape(REQS * LEN, INNER), out_weight, preferred_element_type=jnp.float32).reshape(REQS, LEN, D)
    mixed = (tokens + branch).astype(jnp.bfloat16)
    final_state = jnp.zeros_like(last).at[slot_request].set(last)
    return (mixed, final_state)
```

```python
import functools
import math

import jax
import jax.numpy as jnp
from jax import lax
from jax.experimental import pallas as pl
from jax.experimental.pallas import tpu as pltpu
from jax.sharding import PartitionSpec as P

STATE = 16
RANK = 128
GROUP = 8
VMEM_LIMIT = 48 * 1024 * 1024


def silu(v):
    return v / (1.0 + jnp.exp(-v))


def softplus(v):
    return jnp.maximum(v, 0.0) + jnp.log1p(jnp.exp(-jnp.abs(v)))


def scan_kernel(
    length_ref, low_ref, into_ref, outof_ref, inner_ref, zgate_ref, dtw_ref, dtb_ref, alog_ref, skip_ref,
    gated_ref, final_ref, rate_ref, push_ref, out_ref,
):
    span = inner_ref.shape[0]
    block = 128
    length = length_ref[0]

    @pl.loop(0, span // block)
    def _(i):
        rows = pl.ds(pl.multiple_of(i * block, block), block)
        pre = jnp.dot(low_ref[rows, :], dtw_ref[...], preferred_element_type=jnp.float32)
        rate = softplus(pre + dtb_ref[...].astype(jnp.float32))
        place = lax.broadcasted_iota(jnp.int32, rate.shape, 0) + i * block
        rate = jnp.where(place < length, rate, 0.0)
        rate_ref[rows, :] = rate
        push_ref[rows, :] = rate * inner_ref[rows, :].astype(jnp.float32)

    decay = -jnp.exp(alog_ref[...]) * math.log2(math.e)
    state_shape = decay.shape

    def advance(i, state):
        start = pl.multiple_of(i * GROUP, GROUP)
        tile = pl.ds(pl.multiple_of((i // (128 // GROUP)) * 128, 128), 128)
        shift = lax.rem(128 - lax.rem(i, 128 // GROUP) * GROUP, 128)
        into = pltpu.roll(into_ref[:, tile], shift, 1)
        outof = pltpu.roll(outof_ref[:, tile], shift, 1)
        rows = []
        for j in range(GROUP):
            rate = rate_ref[pl.ds(start + j, 1), :]
            push = push_ref[pl.ds(start + j, 1), :]
            factor = jnp.exp2(jnp.broadcast_to(rate, state_shape) * decay)
            state = factor * state + jnp.broadcast_to(push, state_shape) * into[:, j : j + 1]
            rows.append(jnp.sum(state * outof[:, j : j + 1], axis=0, keepdims=True))
        out_ref[pl.ds(start, GROUP), :] = jnp.concatenate(rows, axis=0)
        return state

    final_ref[...] = lax.fori_loop(0, span // GROUP, advance, jnp.zeros(state_shape, jnp.float32))

    @pl.loop(0, span // block)
    def _(i):
        rows = pl.ds(pl.multiple_of(i * block, block), block)
        scanned = out_ref[rows, :] + skip_ref[...] * inner_ref[rows, :].astype(jnp.float32)
        scanned = scanned.astype(jnp.bfloat16).astype(jnp.float32)
        gated_ref[rows, :] = (scanned * silu(zgate_ref[rows, :].astype(jnp.float32))).astype(jnp.bfloat16)


def scan_call(length, low, into, outof, inner, zgate, dtw, dtb, alog, skip):
    span, width = inner.shape
    vmem = pl.BlockSpec(memory_space=pltpu.VMEM)
    return pl.pallas_call(
        scan_kernel,
        out_shape=(
            jax.ShapeDtypeStruct((span, width), jnp.bfloat16),
            jax.ShapeDtypeStruct((STATE, width), jnp.float32),
        ),
        in_specs=[pl.BlockSpec(memory_space=pltpu.SMEM)] + [vmem] * 9,
        out_specs=(vmem, vmem),
        scratch_shapes=[pltpu.VMEM((span, width), jnp.float32)] * 3,
        compiler_params=pltpu.CompilerParams(vmem_limit_bytes=VMEM_LIMIT),
        cost_estimate=pl.CostEstimate(
            flops=span * width * STATE * 7, bytes_accessed=span * width * 8, transcendentals=span * width * STATE
        ),
        name="scan",
    )(length, low, into, outof, inner, zgate, dtw, dtb, alog, skip)


def per_device(
    hidden,
    lengths,
    slot_request,
    norm_gain,
    in_weight,
    conv_weight,
    conv_bias,
    xproj_weight,
    dt_weight,
    dt_bias,
    a_log,
    skip_gain,
    out_weight,
):
    seq_count = lax.axis_size("seq")
    seq_index = lax.axis_index("seq")
    req_index = lax.axis_index("req")
    rows = hidden.shape[1]
    span = rows * seq_count
    width = in_weight.shape[2]
    taps_count = conv_weight.shape[0]
    tokens = hidden[0].astype(jnp.float32)
    scale = lax.rsqrt(jnp.mean(tokens * tokens, axis=-1, keepdims=True) + 1e-05)
    normed = (tokens * scale * norm_gain.astype(jnp.float32)).astype(jnp.bfloat16)
    w_in = lax.all_gather(in_weight, "req", axis=1, tiled=True)
    w_flat = jnp.concatenate((w_in[0], w_in[1]), axis=1)
    both = jnp.dot(
        lax.all_gather(normed, "seq", axis=0, tiled=True),
        w_flat,
        preferred_element_type=jnp.float32,
    )
    xin = both[:, :width]
    zgate = both[:, width:].astype(jnp.bfloat16)
    padded = jnp.pad(xin, ((taps_count - 1, 0), (0, 0)))
    taps = conv_weight.astype(jnp.float32)
    convolved = conv_bias.astype(jnp.float32) + jnp.zeros_like(xin)
    for tap in range(taps_count):
        convolved = convolved + taps[tap] * padded[tap : tap + span, :]
    inner = jax.nn.silu(convolved).astype(jnp.bfloat16)
    partial_proj = jnp.dot(inner, xproj_weight, preferred_element_type=jnp.float32)
    summed = lax.psum(partial_proj, "seq")
    w_out = lax.all_gather(out_weight, "req", axis=1, tiled=True)
    length_here = lax.dynamic_slice_in_dim(lengths, req_index, 1, 0)
    low = summed[:, :RANK].astype(jnp.bfloat16)
    into = summed[:, RANK : RANK + STATE].T
    outof = summed[:, RANK + STATE :].T
    alog = lax.dynamic_slice_in_dim(a_log, seq_index * width, width, 1)
    skip = lax.dynamic_slice_in_dim(skip_gain, seq_index * width, width, 0)[None]
    gated_ch, mine = scan_call(
        length_here, low, into, outof, inner, zgate, dt_weight, dt_bias[None], alog, skip
    )
    branch = lax.psum_scatter(
        jnp.dot(gated_ch, w_out, preferred_element_type=jnp.float32).astype(jnp.bfloat16),
        "seq",
        scatter_dimension=0,
        tiled=True,
    ).astype(jnp.float32)
    slot_all = lax.all_gather(mine[None], "req", axis=0, tiled=True)
    picked = (slot_request == req_index).astype(jnp.float32)
    final_state = jnp.sum(picked[:, None, None] * slot_all, axis=0, keepdims=True)
    mixed = (tokens + branch).astype(jnp.bfloat16)[None]
    return (mixed, final_state)


def solution(mesh):
    in_specs = (
        P("req", "seq", None),
        P(),
        P(),
        P(),
        P(None, "req", "seq"),
        P(None, "seq"),
        P("seq"),
        P("seq", None),
        P(None, "seq"),
        P("seq"),
        P(),
        P(),
        P("seq", "req"),
    )
    out_specs = (P("req", "seq", None), P("req", None, "seq"))
    return jax.shard_map(
        per_device, mesh=mesh, in_specs=in_specs, out_specs=out_specs, check_vma=False
    )
```

```python
import functools
import math

import jax
import jax.numpy as jnp
from jax import lax
from jax.experimental import pallas as pl
from jax.experimental.pallas import tpu as pltpu
from jax.sharding import PartitionSpec as P

STATE = 16
RANK = 128
GROUP = 8
VMEM_LIMIT = 48 * 1024 * 1024


def silu(v):
    return v / (1.0 + jnp.exp(-v))


def softplus(v):
    return jnp.maximum(v, 0.0) + jnp.log1p(jnp.exp(-jnp.abs(v)))


def scan_kernel(
    length_ref, low_ref, into_ref, outof_ref, inner_ref, zgate_ref, dtw_ref, dtb_ref, alog_ref, skip_ref,
    gated_ref, final_ref, rate_ref, push_ref, out_ref,
):
    span = inner_ref.shape[0]
    block = 128
    length = length_ref[0]

    @pl.loop(0, span // block)
    def _(i):
        rows = pl.ds(pl.multiple_of(i * block, block), block)
        pre = jnp.dot(low_ref[rows, :], dtw_ref[...], preferred_element_type=jnp.float32)
        rate = softplus(pre + dtb_ref[...].astype(jnp.float32))
        place = lax.broadcasted_iota(jnp.int32, rate.shape, 0) + i * block
        rate = jnp.where(place < length, rate, 0.0)
        rate_ref[rows, :] = rate
        push_ref[rows, :] = rate * inner_ref[rows, :].astype(jnp.float32)

    decay = -jnp.exp(alog_ref[...]) * math.log2(math.e)
    state_shape = decay.shape

    def advance(i, state):
        start = pl.multiple_of(i * GROUP, GROUP)
        tile = pl.ds(pl.multiple_of((i // (128 // GROUP)) * 128, 128), 128)
        shift = lax.rem(128 - lax.rem(i, 128 // GROUP) * GROUP, 128)
        into = pltpu.roll(into_ref[:, tile], shift, 1)
        outof = pltpu.roll(outof_ref[:, tile], shift, 1)
        rows = []
        for j in range(GROUP):
            rate = rate_ref[pl.ds(start + j, 1), :]
            push = push_ref[pl.ds(start + j, 1), :]
            factor = jnp.exp2(jnp.broadcast_to(rate, state_shape) * decay)
            state = factor * state + jnp.broadcast_to(push, state_shape) * into[:, j : j + 1]
            rows.append(jnp.sum(state * outof[:, j : j + 1], axis=0, keepdims=True))
        out_ref[pl.ds(start, GROUP), :] = jnp.concatenate(rows, axis=0)
        return state

    final_ref[...] = lax.fori_loop(0, span // GROUP, advance, jnp.zeros(state_shape, jnp.float32))

    @pl.loop(0, span // block)
    def _(i):
        rows = pl.ds(pl.multiple_of(i * block, block), block)
        scanned = out_ref[rows, :] + skip_ref[...] * inner_ref[rows, :].astype(jnp.float32)
        scanned = scanned.astype(jnp.bfloat16).astype(jnp.float32)
        gated_ref[rows, :] = (scanned * silu(zgate_ref[rows, :].astype(jnp.float32))).astype(jnp.bfloat16)


def scan_call(length, low, into, outof, inner, zgate, dtw, dtb, alog, skip):
    span, width = inner.shape
    vmem = pl.BlockSpec(memory_space=pltpu.VMEM)
    return pl.pallas_call(
        scan_kernel,
        out_shape=(
            jax.ShapeDtypeStruct((span, width), jnp.bfloat16),
            jax.ShapeDtypeStruct((STATE, width), jnp.float32),
        ),
        in_specs=[pl.BlockSpec(memory_space=pltpu.SMEM)] + [vmem] * 9,
        out_specs=(vmem, vmem),
        scratch_shapes=[pltpu.VMEM((span, width), jnp.float32)] * 3,
        compiler_params=pltpu.CompilerParams(vmem_limit_bytes=VMEM_LIMIT),
        cost_estimate=pl.CostEstimate(
            flops=span * width * STATE * 7, bytes_accessed=span * width * 8, transcendentals=span * width * STATE
        ),
        name="scan",
    )(length, low, into, outof, inner, zgate, dtw, dtb, alog, skip)


def ring_place(index, count):
    half = count // 2
    y, z = index % 2, index // 2
    return y * (2 * half - 1) + z * (1 - 2 * y)


def ring_index(place, count):
    half = count // 2
    y = place // half
    return 2 * (place * (1 - 2 * y) + y * (2 * half - 1)) + y


def greet(peers):
    barrier = pltpu.get_barrier_semaphore()
    for peer in peers:
        pl.semaphore_signal(barrier, inc=1, device_id=peer, device_id_type=pl.DeviceIdType.MESH)
    pl.semaphore_wait(barrier, len(peers))


def remote(src, dst, send, recv, peer):
    return pltpu.make_async_remote_copy(
        src_ref=src, dst_ref=dst, send_sem=send, recv_sem=recv, device_id=peer,
        device_id_type=pl.DeviceIdType.MESH,
    )


def gather_kernel(
    n, m, normed_ref, win_ref, wout_ref, act_ref, wg_ref, og_ref,
    ring_send, ring_recv, x_send, x_recv, c_send, c_recv, local_sem,
):
    rows = normed_ref.shape[0]
    half = rows // 2
    depth = win_ref.shape[1]
    req, seq = lax.axis_index("req"), lax.axis_index("seq")
    place = ring_place(seq, n)
    right = (req, ring_index((place + 1) % n, n))
    left = (req, ring_index((place + n - 1) % n, n))
    chips = m // 2
    chip, core = req // 2, req % 2
    ahead = (((chip + 1) % chips) * 2 + core, seq)
    behind = (((chip + chips - 1) % chips) * 2 + core, seq)
    mate = (chip * 2 + 1 - core, seq)
    greet([left, right, mate, ahead] + ([behind] if chips > 2 else []))

    def win_at(owner):
        return wg_ref.at[:, pl.ds(pl.multiple_of(owner * depth, depth), depth), :]

    def wout_at(owner):
        return og_ref.at[:, pl.ds(pl.multiple_of(owner * depth, depth), depth)]

    pending = []
    crossing = []
    for which, (src, at) in enumerate(((win_ref, win_at), (wout_ref, wout_at))):
        crossing.append(remote(src, at(req), x_send.at[which, 0], x_recv.at[which, 0], ahead))
        crossing[-1].start()
        own = remote(src, at(req), c_send.at[which, 0], c_recv.at[which, 0], mate)
        own.start()
        pending.append(own)
    locals_ = [
        pltpu.make_async_copy(normed_ref, act_ref.at[seq], local_sem.at[0]),
        pltpu.make_async_copy(win_ref, win_at(req), local_sem.at[1]),
        pltpu.make_async_copy(wout_ref, wout_at(req), local_sem.at[2]),
    ]
    for copy in locals_:
        copy.start()

    ring = []
    for step in range(n - 1):
        pair = []
        for way in range(2):
            part = pl.ds(way * half, half)
            turn = place + (n - step if way == 0 else step)
            owner = ring_index(turn % n, n)
            src = normed_ref.at[part] if step == 0 else act_ref.at[owner, part]
            copy = remote(
                src, act_ref.at[owner, part], ring_send.at[way, step], ring_recv.at[way, step],
                right if way == 0 else left,
            )
            copy.start()
            pair.append(copy)
        if step == n - 2:
            for hop in range(1, chips):
                owner = ((chip + chips - hop) % chips) * 2 + core
                coming = crossing
                crossing = []
                for which, at in enumerate((win_at, wout_at)):
                    coming[which].wait()
                    block = at(owner)
                    passed = remote(block, block, c_send.at[which, hop], c_recv.at[which, hop], mate)
                    passed.start()
                    pending.append(passed)
                    if hop < chips - 1:
                        crossing.append(remote(block, block, x_send.at[which, hop], x_recv.at[which, hop], ahead))
                        crossing[-1].start()
        for copy in pair:
            copy.wait_recv()
        ring += pair
    for copy in ring:
        copy.wait_send()
    for copy in pending:
        copy.wait()
    for copy in locals_:
        copy.wait()


def gather_call(n, m, normed, win, wout):
    rows, model = normed.shape
    _, depth, width = win.shape
    anywhere = pl.BlockSpec(memory_space=pl.ANY)
    dma = pltpu.SemaphoreType.DMA
    return pl.pallas_call(
        functools.partial(gather_kernel, n, m),
        out_shape=(
            jax.ShapeDtypeStruct((n, rows, model), jnp.bfloat16),
            jax.ShapeDtypeStruct((2, depth * m, width), jnp.bfloat16),
            jax.ShapeDtypeStruct((width, depth * m), jnp.bfloat16),
        ),
        in_specs=[anywhere] * 3,
        out_specs=(anywhere,) * 3,
        scratch_shapes=[
            dma((2, n - 1)), dma((2, n - 1)), dma((2, m // 2 - 1)), dma((2, m // 2 - 1)),
            dma((2, m // 2)), dma((2, m // 2)), dma((3,)),
        ],
        compiler_params=pltpu.CompilerParams(
            collective_id=0, has_side_effects=True, vmem_limit_bytes=VMEM_LIMIT
        ),
        name="gather",
    )(normed, win, wout)


def total_kernel(n, part_ref, sum_ref, send_buf, recv_buf, own_buf, send, recv, send2, recv2):
    req, seq = lax.axis_index("req"), lax.axis_index("seq")
    peers = [(req, (seq + d) % n) for d in range(1, n)]
    greet(peers)
    send_buf[...] = part_ref[...].astype(jnp.bfloat16)
    first = []
    for d in range(1, n):
        copy = remote(
            send_buf.at[(seq + d) % n], recv_buf.at[d - 1], send.at[d - 1], recv.at[d - 1], peers[d - 1]
        )
        copy.start()
        first.append(copy)
    total = part_ref[seq]
    for d in range(1, n):
        first[d - 1].wait_recv()
        total = total + recv_buf[d - 1].astype(jnp.float32)
    own_buf[...] = total.astype(jnp.bfloat16)
    sum_ref[seq] = own_buf[...]
    second = []
    for d in range(1, n):
        copy = remote(own_buf, sum_ref.at[seq], send2.at[d - 1], recv2.at[d - 1], peers[d - 1])
        copy.start()
        second.append(copy)
    for copy in second:
        copy.wait()
    for copy in first:
        copy.wait_send()


def total_call(n, part):
    vmem = pl.BlockSpec(memory_space=pltpu.VMEM)
    dma = pltpu.SemaphoreType.DMA
    _, rows, columns = part.shape
    return pl.pallas_call(
        functools.partial(total_kernel, n),
        out_shape=jax.ShapeDtypeStruct(part.shape, jnp.bfloat16),
        in_specs=[vmem],
        out_specs=vmem,
        scratch_shapes=[
            pltpu.VMEM((n, rows, columns), jnp.bfloat16),
            pltpu.VMEM((n - 1, rows, columns), jnp.bfloat16),
            pltpu.VMEM((rows, columns), jnp.bfloat16),
        ] + [dma((n - 1,))] * 4,
        compiler_params=pltpu.CompilerParams(
            collective_id=1, has_side_effects=True, vmem_limit_bytes=VMEM_LIMIT
        ),
        name="total",
    )(part)


def output_kernel(
    n, m, gated_ref, wout_ref, hidden_ref, state_ref, mixed_ref, slots_ref,
    send_buf, recv_buf, acc_ref, send, recv, state_send, state_recv,
):
    rows, model = hidden_ref.shape
    half = model // 2
    req, seq = lax.axis_index("req"), lax.axis_index("seq")
    place = ring_place(seq, n)
    right = (req, ring_index((place + 1) % n, n))
    left = (req, ring_index((place + n - 1) % n, n))
    peers = [((req + d) % m, seq) for d in range(1, m)]
    greet([left, right] + peers)
    states = []
    for d in range(1, m):
        copy = remote(state_ref, slots_ref.at[req], state_send.at[d - 1], state_recv.at[d - 1], peers[d - 1])
        copy.start()
        states.append(copy)
    slots_ref[req] = state_ref[...]

    def hop(way, step):
        return remote(
            send_buf.at[way, step], recv_buf.at[way, step], send.at[way, step], recv.at[way, step],
            right if way == 0 else left,
        )

    def product(way, step):
        turn = place + (2 * n - 1 - step if way == 0 else 1 + step)
        owner = ring_index(turn % n, n)
        block = gated_ref[pl.ds(pl.multiple_of(owner * rows, rows), rows), :]
        acc_ref[way] = jnp.dot(
            block, wout_ref[:, way * half : (way + 1) * half], preferred_element_type=jnp.float32
        )

    for way in range(2):
        product(way, 0)
        send_buf[way, 0] = acc_ref[way].astype(jnp.bfloat16)
        hop(way, 0).start()

    def middle(step, carry):
        for way in range(2):
            product(way, step)
        for way in range(2):
            hop(way, step - 1).wait_recv()
            send_buf[way, step] = (acc_ref[way] + recv_buf[way, step - 1].astype(jnp.float32)).astype(jnp.bfloat16)
            hop(way, step).start()
        return carry

    lax.fori_loop(1, n - 1, middle, 0)
    for way in range(2):
        product(way, n - 1)
    for way in range(2):
        hop(way, n - 2).wait_recv()
        columns = slice(way * half, (way + 1) * half)
        branch = acc_ref[way] + recv_buf[way, n - 2].astype(jnp.float32)
        mixed_ref[:, columns] = (hidden_ref[:, columns].astype(jnp.float32) + branch).astype(jnp.bfloat16)
    for step in range(n - 1):
        for way in range(2):
            hop(way, step).wait_send()
    for copy in states:
        copy.wait()


def output_call(n, m, gated, wout, hidden, state):
    rows, model = hidden.shape
    vmem = pl.BlockSpec(memory_space=pltpu.VMEM)
    dma = pltpu.SemaphoreType.DMA
    return pl.pallas_call(
        functools.partial(output_kernel, n, m),
        out_shape=(
            jax.ShapeDtypeStruct((rows, model), jnp.bfloat16),
            jax.ShapeDtypeStruct((m,) + state.shape, jnp.float32),
        ),
        in_specs=[vmem] * 4,
        out_specs=(vmem, vmem),
        scratch_shapes=[
            pltpu.VMEM((2, n - 1, rows, model // 2), jnp.bfloat16),
            pltpu.VMEM((2, n - 1, rows, model // 2), jnp.bfloat16),
            pltpu.VMEM((2, rows, model // 2), jnp.float32),
            dma((2, n - 1)), dma((2, n - 1)), dma((m - 1,)), dma((m - 1,)),
        ],
        compiler_params=pltpu.CompilerParams(
            collective_id=2, has_side_effects=True, vmem_limit_bytes=VMEM_LIMIT
        ),
        name="output",
    )(gated, wout, hidden, state)


def per_device(
    hidden,
    lengths,
    slot_request,
    norm_gain,
    in_weight,
    conv_weight,
    conv_bias,
    xproj_weight,
    dt_weight,
    dt_bias,
    a_log,
    skip_gain,
    out_weight,
):
    seq_count = lax.axis_size("seq")
    seq_index = lax.axis_index("seq")
    req_index = lax.axis_index("req")
    rows = hidden.shape[1]
    span = rows * seq_count
    width = in_weight.shape[2]
    taps_count = conv_weight.shape[0]
    tokens = hidden[0].astype(jnp.float32)
    scale = lax.rsqrt(jnp.mean(tokens * tokens, axis=-1, keepdims=True) + 1e-05)
    normed = (tokens * scale * norm_gain.astype(jnp.float32)).astype(jnp.bfloat16)
    req_count = lax.axis_size("req")
    act, w_in, w_out = gather_call(seq_count, req_count, normed, in_weight, out_weight)
    act = act.reshape(span, -1)
    xin = jnp.dot(act, w_in[0], preferred_element_type=jnp.float32)
    zgate = jnp.dot(act, w_in[1], preferred_element_type=jnp.float32).astype(jnp.bfloat16)
    padded = jnp.pad(xin, ((taps_count - 1, 0), (0, 0)))
    taps = conv_weight.astype(jnp.float32)
    convolved = conv_bias.astype(jnp.float32) + jnp.zeros_like(xin)
    for tap in range(taps_count):
        convolved = convolved + taps[tap] * padded[tap : tap + span, :]
    inner = jax.nn.silu(convolved).astype(jnp.bfloat16)
    partial_proj = jnp.dot(inner, xproj_weight, preferred_element_type=jnp.float32)
    summed = total_call(seq_count, partial_proj.reshape(seq_count, rows, -1)).reshape(span, -1)
    length_here = lax.dynamic_slice_in_dim(lengths, req_index, 1, 0)
    low = summed[:, :RANK]
    into = summed[:, RANK : RANK + STATE].astype(jnp.float32).T
    outof = summed[:, RANK + STATE :].astype(jnp.float32).T
    alog = lax.dynamic_slice_in_dim(a_log, seq_index * width, width, 1)
    skip = lax.dynamic_slice_in_dim(skip_gain, seq_index * width, width, 0)[None]
    gated_ch, mine = scan_call(
        length_here, low, into, outof, inner, zgate, dt_weight, dt_bias[None], alog, skip
    )
    mixed, slot_all = output_call(seq_count, req_count, gated_ch, w_out, hidden[0], mine)
    picked = (slot_request == req_index).astype(jnp.float32)
    final_state = jnp.sum(picked[:, None, None] * slot_all, axis=0, keepdims=True)
    return (mixed[None], final_state)


def solution(mesh):
    in_specs = (
        P("req", "seq", None),
        P(),
        P(),
        P(),
        P(None, "req", "seq"),
        P(None, "seq"),
        P("seq"),
        P("seq", None),
        P(None, "seq"),
        P("seq"),
        P(),
        P(),
        P("seq", "req"),
    )
    out_specs = (P("req", "seq", None), P("req", None, "seq"))
    return jax.shard_map(
        per_device, mesh=mesh, in_specs=in_specs, out_specs=out_specs, check_vma=False
    )
```

```python
import functools
import math

import jax
import jax.numpy as jnp
from jax import lax
from jax.experimental import pallas as pl
from jax.experimental.pallas import tpu as pltpu
from jax.sharding import PartitionSpec as P

STATE = 16
RANK = 128
GROUP = 8
VMEM_LIMIT = 48 * 1024 * 1024


def silu(v):
    return v / (1.0 + jnp.exp(-v))


def softplus(v):
    return jnp.maximum(v, 0.0) + jnp.log1p(jnp.exp(-jnp.abs(v)))


def scan_kernel(
    length_ref, sums_ref, inner_ref, zgate_ref, dtw_ref, dtb_ref, alog_ref, skip_ref,
    gated_ref, final_ref, rate_ref, push_ref, out_ref,
):
    blocks, _, rows = sums_ref.shape
    length = length_ref[0]
    decay = -jnp.exp(alog_ref[...]) * math.log2(math.e)
    state_shape = decay.shape

    def advance(i, state):
        here = pl.ds(pl.multiple_of(i * rows, rows), rows)
        low = sums_ref[i, :RANK, :].astype(jnp.float32).T.astype(jnp.bfloat16)
        pre = jnp.dot(low, dtw_ref[...], preferred_element_type=jnp.float32)
        rates = softplus(pre + dtb_ref[...].astype(jnp.float32))
        place = lax.broadcasted_iota(jnp.int32, rates.shape, 0) + i * rows
        rates = jnp.where(place < length, rates, 0.0)
        rate_ref[...] = rates
        push_ref[...] = rates * inner_ref[here, :].astype(jnp.float32)
        into = sums_ref[i, RANK : RANK + STATE, :].astype(jnp.float32)
        outof = sums_ref[i, RANK + STATE :, :].astype(jnp.float32)
        for start in range(0, rows, GROUP):
            lines = []
            for t in range(start, start + GROUP):
                rate = rate_ref[t : t + 1, :]
                push = push_ref[t : t + 1, :]
                factor = jnp.exp2(jnp.broadcast_to(rate, state_shape) * decay)
                state = factor * state + jnp.broadcast_to(push, state_shape) * into[:, t : t + 1]
                lines.append(jnp.sum(state * outof[:, t : t + 1], axis=0, keepdims=True))
            out_ref[start : start + GROUP, :] = jnp.concatenate(lines, axis=0)
        scanned = out_ref[...] + skip_ref[...] * inner_ref[here, :].astype(jnp.float32)
        scanned = scanned.astype(jnp.bfloat16).astype(jnp.float32)
        gated_ref[here, :] = (scanned * silu(zgate_ref[here, :].astype(jnp.float32))).astype(jnp.bfloat16)
        return state

    final_ref[...] = lax.fori_loop(0, blocks, advance, jnp.zeros(state_shape, jnp.float32))


def scan_call(length, sums, inner, zgate, dtw, dtb, alog, skip):
    span, width = inner.shape
    vmem = pl.BlockSpec(memory_space=pltpu.VMEM)
    return pl.pallas_call(
        scan_kernel,
        out_shape=(
            jax.ShapeDtypeStruct((span, width), jnp.bfloat16),
            jax.ShapeDtypeStruct((STATE, width), jnp.float32),
        ),
        in_specs=[pl.BlockSpec(memory_space=pltpu.SMEM)] + [vmem] * 7,
        out_specs=(vmem, vmem),
        scratch_shapes=[pltpu.VMEM((sums.shape[2], width), jnp.float32)] * 3,
        compiler_params=pltpu.CompilerParams(vmem_limit_bytes=VMEM_LIMIT),
        cost_estimate=pl.CostEstimate(
            flops=span * width * STATE * 7, bytes_accessed=span * width * 8, transcendentals=span * width * STATE
        ),
        name="scan",
    )(length, sums, inner, zgate, dtw, dtb, alog, skip)


def ring_place(index, count):
    half = count // 2
    y, z = index % 2, index // 2
    return y * (2 * half - 1) + z * (1 - 2 * y)


def ring_index(place, count):
    half = count // 2
    y = place // half
    return 2 * (place * (1 - 2 * y) + y * (2 * half - 1)) + y


def greet(peers):
    barrier = pltpu.get_barrier_semaphore()
    for peer in peers:
        pl.semaphore_signal(barrier, inc=1, device_id=peer, device_id_type=pl.DeviceIdType.MESH)
    pl.semaphore_wait(barrier, len(peers))


def remote(src, dst, send, recv, peer):
    return pltpu.make_async_remote_copy(
        src_ref=src, dst_ref=dst, send_sem=send, recv_sem=recv, device_id=peer,
        device_id_type=pl.DeviceIdType.MESH,
    )


def gather_kernel(
    n, m, normed_ref, win_ref, wout_ref, act_ref, wg_ref, og_ref,
    ring_send, ring_recv, x_send, x_recv, c_send, c_recv, local_sem,
):
    rows = normed_ref.shape[0]
    half = rows // 2
    depth = win_ref.shape[1]
    req, seq = lax.axis_index("req"), lax.axis_index("seq")
    place = ring_place(seq, n)
    right = (req, ring_index((place + 1) % n, n))
    left = (req, ring_index((place + n - 1) % n, n))
    chips = m // 2
    chip, core = req // 2, req % 2
    ahead = (((chip + 1) % chips) * 2 + core, seq)
    behind = (((chip + chips - 1) % chips) * 2 + core, seq)
    mate = (chip * 2 + 1 - core, seq)
    greet([left, right, mate, ahead] + ([behind] if chips > 2 else []))

    def win_at(owner):
        return wg_ref.at[:, pl.ds(pl.multiple_of(owner * depth, depth), depth), :]

    def wout_at(owner):
        return og_ref.at[:, pl.ds(pl.multiple_of(owner * depth, depth), depth)]

    pending = []
    crossing = []
    for which, (src, at) in enumerate(((win_ref, win_at), (wout_ref, wout_at))):
        crossing.append(remote(src, at(req), x_send.at[which, 0], x_recv.at[which, 0], ahead))
        crossing[-1].start()
        own = remote(src, at(req), c_send.at[which, 0], c_recv.at[which, 0], mate)
        own.start()
        pending.append(own)
    locals_ = [
        pltpu.make_async_copy(normed_ref, act_ref.at[seq], local_sem.at[0]),
        pltpu.make_async_copy(win_ref, win_at(req), local_sem.at[1]),
        pltpu.make_async_copy(wout_ref, wout_at(req), local_sem.at[2]),
    ]
    for copy in locals_:
        copy.start()

    ring = []
    for step in range(n - 1):
        pair = []
        for way in range(2):
            part = pl.ds(way * half, half)
            turn = place + (n - step if way == 0 else step)
            owner = ring_index(turn % n, n)
            src = normed_ref.at[part] if step == 0 else act_ref.at[owner, part]
            copy = remote(
                src, act_ref.at[owner, part], ring_send.at[way, step], ring_recv.at[way, step],
                right if way == 0 else left,
            )
            copy.start()
            pair.append(copy)
        if step == n - 2:
            for hop in range(1, chips):
                owner = ((chip + chips - hop) % chips) * 2 + core
                coming = crossing
                crossing = []
                for which, at in enumerate((win_at, wout_at)):
                    coming[which].wait()
                    block = at(owner)
                    passed = remote(block, block, c_send.at[which, hop], c_recv.at[which, hop], mate)
                    passed.start()
                    pending.append(passed)
                    if hop < chips - 1:
                        crossing.append(remote(block, block, x_send.at[which, hop], x_recv.at[which, hop], ahead))
                        crossing[-1].start()
        for copy in pair:
            copy.wait_recv()
        ring += pair
    for copy in ring:
        copy.wait_send()
    for copy in pending:
        copy.wait()
    for copy in locals_:
        copy.wait()


def gather_call(n, m, normed, win, wout):
    rows, model = normed.shape
    _, depth, width = win.shape
    anywhere = pl.BlockSpec(memory_space=pl.ANY)
    dma = pltpu.SemaphoreType.DMA
    return pl.pallas_call(
        functools.partial(gather_kernel, n, m),
        out_shape=(
            jax.ShapeDtypeStruct((n, rows, model), jnp.bfloat16),
            jax.ShapeDtypeStruct((2, depth * m, width), jnp.bfloat16),
            jax.ShapeDtypeStruct((width, depth * m), jnp.bfloat16),
        ),
        in_specs=[anywhere] * 3,
        out_specs=(anywhere,) * 3,
        scratch_shapes=[
            dma((2, n - 1)), dma((2, n - 1)), dma((2, m // 2 - 1)), dma((2, m // 2 - 1)),
            dma((2, m // 2)), dma((2, m // 2)), dma((3,)),
        ],
        compiler_params=pltpu.CompilerParams(
            collective_id=0, has_side_effects=True, vmem_limit_bytes=VMEM_LIMIT
        ),
        name="gather",
    )(normed, win, wout)


def total_kernel(n, inner_ref, weight_ref, sum_ref, send_buf, recv_buf, own_buf, send, recv, send2, recv2):
    req, seq = lax.axis_index("req"), lax.axis_index("seq")
    rows = inner_ref.shape[0] // n
    peers = [(req, (seq + d) % n) for d in range(1, n)]

    def partial(owner):
        block = inner_ref[pl.ds(pl.multiple_of(owner * rows, rows), rows), :]
        return lax.dot_general(
            weight_ref[...], block, (((1,), (1,)), ((), ())), preferred_element_type=jnp.float32
        )

    greet(peers)
    first = []
    for d in range(1, n):
        send_buf[d - 1] = partial((seq + d) % n).astype(jnp.bfloat16)
        copy = remote(send_buf.at[d - 1], recv_buf.at[d - 1], send.at[d - 1], recv.at[d - 1], peers[d - 1])
        copy.start()
        first.append(copy)
    total = partial(seq)
    for d in range(1, n):
        first[d - 1].wait_recv()
        total = total + recv_buf[d - 1].astype(jnp.float32)
    own_buf[...] = total.astype(jnp.bfloat16)
    second = []
    for d in range(1, n):
        copy = remote(own_buf, sum_ref.at[seq], send2.at[d - 1], recv2.at[d - 1], peers[d - 1])
        copy.start()
        second.append(copy)
    sum_ref[seq] = own_buf[...]
    for copy in second:
        copy.wait()
    for copy in first:
        copy.wait_send()


def total_call(n, inner, weight):
    vmem = pl.BlockSpec(memory_space=pltpu.VMEM)
    dma = pltpu.SemaphoreType.DMA
    columns, rows = weight.shape[0], inner.shape[0] // n
    return pl.pallas_call(
        functools.partial(total_kernel, n),
        out_shape=jax.ShapeDtypeStruct((n, columns, rows), jnp.bfloat16),
        in_specs=[vmem, vmem],
        out_specs=vmem,
        scratch_shapes=[
            pltpu.VMEM((n - 1, columns, rows), jnp.bfloat16),
            pltpu.VMEM((n - 1, columns, rows), jnp.bfloat16),
            pltpu.VMEM((columns, rows), jnp.bfloat16),
        ] + [dma((n - 1,))] * 4,
        compiler_params=pltpu.CompilerParams(
            collective_id=1, has_side_effects=True, vmem_limit_bytes=VMEM_LIMIT
        ),
        name="total",
    )(inner, weight)


def output_kernel(
    n, m, gated_ref, wout_ref, hidden_ref, state_ref, mixed_ref, slots_ref,
    send_buf, recv_buf, acc_ref, send, recv, state_send, state_recv,
):
    rows, model = hidden_ref.shape
    half = model // 2
    req, seq = lax.axis_index("req"), lax.axis_index("seq")
    place = ring_place(seq, n)
    right = (req, ring_index((place + 1) % n, n))
    left = (req, ring_index((place + n - 1) % n, n))
    peers = [((req + d) % m, seq) for d in range(1, m)]
    greet([left, right] + peers)
    states = []
    for d in range(1, m):
        copy = remote(state_ref, slots_ref.at[req], state_send.at[d - 1], state_recv.at[d - 1], peers[d - 1])
        copy.start()
        states.append(copy)
    slots_ref[req] = state_ref[...]

    def hop(way, step):
        return remote(
            send_buf.at[way, step], recv_buf.at[way, step], send.at[way, step], recv.at[way, step],
            right if way == 0 else left,
        )

    def product(way, step):
        turn = place + (2 * n - 1 - step if way == 0 else 1 + step)
        owner = ring_index(turn % n, n)
        block = gated_ref[pl.ds(pl.multiple_of(owner * rows, rows), rows), :]
        acc_ref[way] = jnp.dot(
            block, wout_ref[:, way * half : (way + 1) * half], preferred_element_type=jnp.float32
        )

    for way in range(2):
        product(way, 0)
        send_buf[way, 0] = acc_ref[way].astype(jnp.bfloat16)
        hop(way, 0).start()

    def middle(step, carry):
        for way in range(2):
            product(way, step)
        for way in range(2):
            hop(way, step - 1).wait_recv()
            send_buf[way, step] = (acc_ref[way] + recv_buf[way, step - 1].astype(jnp.float32)).astype(jnp.bfloat16)
            hop(way, step).start()
        return carry

    lax.fori_loop(1, n - 1, middle, 0)
    for way in range(2):
        product(way, n - 1)
    for way in range(2):
        hop(way, n - 2).wait_recv()
        columns = slice(way * half, (way + 1) * half)
        branch = acc_ref[way] + recv_buf[way, n - 2].astype(jnp.float32)
        mixed_ref[:, columns] = (hidden_ref[:, columns].astype(jnp.float32) + branch).astype(jnp.bfloat16)
    for step in range(n - 1):
        for way in range(2):
            hop(way, step).wait_send()
    for copy in states:
        copy.wait()


def output_call(n, m, gated, wout, hidden, state):
    rows, model = hidden.shape
    vmem = pl.BlockSpec(memory_space=pltpu.VMEM)
    dma = pltpu.SemaphoreType.DMA
    return pl.pallas_call(
        functools.partial(output_kernel, n, m),
        out_shape=(
            jax.ShapeDtypeStruct((rows, model), jnp.bfloat16),
            jax.ShapeDtypeStruct((m,) + state.shape, jnp.float32),
        ),
        in_specs=[vmem] * 4,
        out_specs=(vmem, vmem),
        scratch_shapes=[
            pltpu.VMEM((2, n - 1, rows, model // 2), jnp.bfloat16),
            pltpu.VMEM((2, n - 1, rows, model // 2), jnp.bfloat16),
            pltpu.VMEM((2, rows, model // 2), jnp.float32),
            dma((2, n - 1)), dma((2, n - 1)), dma((m - 1,)), dma((m - 1,)),
        ],
        compiler_params=pltpu.CompilerParams(
            collective_id=2, has_side_effects=True, vmem_limit_bytes=VMEM_LIMIT
        ),
        name="output",
    )(gated, wout, hidden, state)


def per_device(
    hidden,
    lengths,
    slot_request,
    norm_gain,
    in_weight,
    conv_weight,
    conv_bias,
    xproj_weight,
    dt_weight,
    dt_bias,
    a_log,
    skip_gain,
    out_weight,
):
    seq_count = lax.axis_size("seq")
    seq_index = lax.axis_index("seq")
    req_index = lax.axis_index("req")
    rows = hidden.shape[1]
    span = rows * seq_count
    width = in_weight.shape[2]
    taps_count = conv_weight.shape[0]
    tokens = hidden[0].astype(jnp.float32)
    scale = lax.rsqrt(jnp.mean(tokens * tokens, axis=-1, keepdims=True) + 1e-05)
    normed = (tokens * scale * norm_gain.astype(jnp.float32)).astype(jnp.bfloat16)
    req_count = lax.axis_size("req")
    act, w_in, w_out = gather_call(seq_count, req_count, normed, in_weight, out_weight)
    act = act.reshape(span, -1)
    xin = jnp.dot(act, w_in[0], preferred_element_type=jnp.float32)
    zgate = jnp.dot(act, w_in[1], preferred_element_type=jnp.float32).astype(jnp.bfloat16)
    padded = jnp.pad(xin, ((taps_count - 1, 0), (0, 0)))
    taps = conv_weight.astype(jnp.float32)
    convolved = conv_bias.astype(jnp.float32) + jnp.zeros_like(xin)
    for tap in range(taps_count):
        convolved = convolved + taps[tap] * padded[tap : tap + span, :]
    inner = jax.nn.silu(convolved).astype(jnp.bfloat16)
    sums = total_call(seq_count, inner, xproj_weight.T)
    length_here = lax.dynamic_slice_in_dim(lengths, req_index, 1, 0)
    alog = lax.dynamic_slice_in_dim(a_log, seq_index * width, width, 1)
    skip = lax.dynamic_slice_in_dim(skip_gain, seq_index * width, width, 0)[None]
    gated_ch, mine = scan_call(
        length_here, sums, inner, zgate, dt_weight, dt_bias[None], alog, skip
    )
    mixed, slot_all = output_call(seq_count, req_count, gated_ch, w_out, hidden[0], mine)
    picked = (slot_request == req_index).astype(jnp.float32)
    final_state = jnp.sum(picked[:, None, None] * slot_all, axis=0, keepdims=True)
    return (mixed[None], final_state)


def solution(mesh):
    in_specs = (
        P("req", "seq", None),
        P(),
        P(),
        P(),
        P(None, "req", "seq"),
        P(None, "seq"),
        P("seq"),
        P("seq", None),
        P(None, "seq"),
        P("seq"),
        P(),
        P(),
        P("seq", "req"),
    )
    out_specs = (P("req", "seq", None), P("req", None, "seq"))
    return jax.shard_map(
        per_device, mesh=mesh, in_specs=in_specs, out_specs=out_specs, check_vma=False
    )
```

```python
import functools
import math

import jax
import jax.numpy as jnp
from jax import lax
from jax.experimental import pallas as pl
from jax.experimental.pallas import tpu as pltpu
from jax.sharding import PartitionSpec as P

STATE = 16
RANK = 128
GROUP = 8
STREAMS = 4
VMEM_LIMIT = 48 * 1024 * 1024


def silu(v):
    return v / (1.0 + jnp.exp(-v))


def softplus(v):
    return jnp.maximum(v, 0.0) + jnp.log1p(jnp.exp(-jnp.abs(v)))


def scan_kernel(
    length_ref, sums_ref, inner_ref, zgate_ref, dtw_ref, dtb_ref, alog_ref, skip_ref,
    gated_ref, final_ref, rate_ref, push_ref, out_ref,
):
    blocks, _, rows = sums_ref.shape
    length = length_ref[0]
    decay = -jnp.exp(alog_ref[...]) * math.log2(math.e)
    state_shape = decay.shape

    def advance(i, state):
        here = pl.ds(pl.multiple_of(i * rows, rows), rows)
        low = sums_ref[i, :RANK, :].astype(jnp.float32).T.astype(jnp.bfloat16)
        pre = jnp.dot(low, dtw_ref[...], preferred_element_type=jnp.float32)
        rates = softplus(pre + dtb_ref[...].astype(jnp.float32))
        place = lax.broadcasted_iota(jnp.int32, rates.shape, 0) + i * rows
        rates = jnp.where(place < length, rates, 0.0)
        rate_ref[...] = rates
        push_ref[...] = rates * inner_ref[here, :].astype(jnp.float32)
        into = sums_ref[i, RANK : RANK + STATE, :].astype(jnp.float32)
        outof = sums_ref[i, RANK + STATE :, :].astype(jnp.float32)
        for start in range(0, rows, GROUP):
            lines = []
            for t in range(start, start + GROUP):
                rate = rate_ref[t : t + 1, :]
                push = push_ref[t : t + 1, :]
                factor = jnp.exp2(jnp.broadcast_to(rate, state_shape) * decay)
                state = factor * state + jnp.broadcast_to(push, state_shape) * into[:, t : t + 1]
                lines.append(jnp.sum(state * outof[:, t : t + 1], axis=0, keepdims=True))
            out_ref[start : start + GROUP, :] = jnp.concatenate(lines, axis=0)
        scanned = out_ref[...] + skip_ref[...] * inner_ref[here, :].astype(jnp.float32)
        scanned = scanned.astype(jnp.bfloat16).astype(jnp.float32)
        gated_ref[here, :] = (scanned * silu(zgate_ref[here, :].astype(jnp.float32))).astype(jnp.bfloat16)
        return state

    final_ref[...] = lax.fori_loop(0, blocks, advance, jnp.zeros(state_shape, jnp.float32))


def scan_call(length, sums, inner, zgate, dtw, dtb, alog, skip):
    span, width = inner.shape
    vmem = pl.BlockSpec(memory_space=pltpu.VMEM)
    return pl.pallas_call(
        scan_kernel,
        out_shape=(
            jax.ShapeDtypeStruct((span, width), jnp.bfloat16),
            jax.ShapeDtypeStruct((STATE, width), jnp.float32),
        ),
        in_specs=[pl.BlockSpec(memory_space=pltpu.SMEM)] + [vmem] * 7,
        out_specs=(vmem, vmem),
        scratch_shapes=[pltpu.VMEM((sums.shape[2], width), jnp.float32)] * 3,
        compiler_params=pltpu.CompilerParams(vmem_limit_bytes=VMEM_LIMIT),
        cost_estimate=pl.CostEstimate(
            flops=span * width * STATE * 7, bytes_accessed=span * width * 8, transcendentals=span * width * STATE
        ),
        name="scan",
    )(length, sums, inner, zgate, dtw, dtb, alog, skip)


def ring_place(index, count):
    half = count // 2
    y, z = index % 2, index // 2
    return y * (2 * half - 1) + z * (1 - 2 * y)


def ring_index(place, count):
    half = count // 2
    y = place // half
    return 2 * (place * (1 - 2 * y) + y * (2 * half - 1)) + y


def greet(peers):
    barrier = pltpu.get_barrier_semaphore()
    for peer in peers:
        pl.semaphore_signal(barrier, inc=1, device_id=peer, device_id_type=pl.DeviceIdType.MESH)
    pl.semaphore_wait(barrier, len(peers))


def remote(src, dst, send, recv, peer):
    return pltpu.make_async_remote_copy(
        src_ref=src, dst_ref=dst, send_sem=send, recv_sem=recv, device_id=peer,
        device_id_type=pl.DeviceIdType.MESH,
    )


def gather_kernel(
    n, m, normed_ref, win_ref, wout_ref, act_ref, wg_ref, og_ref,
    ring_send, ring_recv, x_send, x_recv, c_send, c_recv, local_sem,
):
    rows = normed_ref.shape[0]
    piece = rows // STREAMS
    depth = win_ref.shape[1]
    req, seq = lax.axis_index("req"), lax.axis_index("seq")
    place = ring_place(seq, n)
    right = (req, ring_index((place + 1) % n, n))
    left = (req, ring_index((place + n - 1) % n, n))
    chips = m // 2
    chip, core = req // 2, req % 2
    ahead = (((chip + 1) % chips) * 2 + core, seq)
    behind = (((chip + chips - 1) % chips) * 2 + core, seq)
    mate = (chip * 2 + 1 - core, seq)
    greet([left, right, mate, ahead] + ([behind] if chips > 2 else []))

    def win_at(owner):
        return wg_ref.at[:, pl.ds(pl.multiple_of(owner * depth, depth), depth), :]

    def wout_at(owner):
        return og_ref.at[:, pl.ds(pl.multiple_of(owner * depth, depth), depth)]

    pending = []
    crossing = []
    for which, (src, at) in enumerate(((win_ref, win_at), (wout_ref, wout_at))):
        crossing.append(remote(src, at(req), x_send.at[which, 0], x_recv.at[which, 0], ahead))
        crossing[-1].start()
        own = remote(src, at(req), c_send.at[which, 0], c_recv.at[which, 0], mate)
        own.start()
        pending.append(own)
    locals_ = [
        pltpu.make_async_copy(normed_ref, act_ref.at[seq], local_sem.at[0]),
        pltpu.make_async_copy(win_ref, win_at(req), local_sem.at[1]),
        pltpu.make_async_copy(wout_ref, wout_at(req), local_sem.at[2]),
    ]
    for copy in locals_:
        copy.start()

    ring = []
    latest = [None] * STREAMS
    for step in range(n - 1):
        for way in range(STREAMS):
            part = pl.ds(way * piece, piece)
            turn = place + (n - step if way % 2 == 0 else step)
            owner = ring_index(turn % n, n)
            src = normed_ref.at[part] if step == 0 else act_ref.at[owner, part]
            copy = remote(
                src, act_ref.at[owner, part], ring_send.at[way, step], ring_recv.at[way, step],
                right if way % 2 == 0 else left,
            )
            if step > 0:
                latest[way].wait_recv()
            copy.start()
            latest[way] = copy
            ring.append(copy)
        if step == n - 2:
            for hop in range(1, chips):
                owner = ((chip + chips - hop) % chips) * 2 + core
                coming = crossing
                crossing = []
                for which, at in enumerate((win_at, wout_at)):
                    coming[which].wait()
                    block = at(owner)
                    passed = remote(block, block, c_send.at[which, hop], c_recv.at[which, hop], mate)
                    passed.start()
                    pending.append(passed)
                    if hop < chips - 1:
                        crossing.append(remote(block, block, x_send.at[which, hop], x_recv.at[which, hop], ahead))
                        crossing[-1].start()
    for copy in latest:
        copy.wait_recv()
    for copy in ring:
        copy.wait_send()
    for copy in pending:
        copy.wait()
    for copy in locals_:
        copy.wait()


def gather_call(n, m, normed, win, wout):
    rows, model = normed.shape
    _, depth, width = win.shape
    anywhere = pl.BlockSpec(memory_space=pl.ANY)
    dma = pltpu.SemaphoreType.DMA
    return pl.pallas_call(
        functools.partial(gather_kernel, n, m),
        out_shape=(
            jax.ShapeDtypeStruct((n, rows, model), jnp.bfloat16),
            jax.ShapeDtypeStruct((2, depth * m, width), jnp.bfloat16),
            jax.ShapeDtypeStruct((width, depth * m), jnp.bfloat16),
        ),
        in_specs=[anywhere] * 3,
        out_specs=(anywhere,) * 3,
        scratch_shapes=[
            dma((STREAMS, n - 1)), dma((STREAMS, n - 1)), dma((2, m // 2 - 1)), dma((2, m // 2 - 1)),
            dma((2, m // 2)), dma((2, m // 2)), dma((3,)),
        ],
        compiler_params=pltpu.CompilerParams(
            collective_id=0, has_side_effects=True, vmem_limit_bytes=VMEM_LIMIT
        ),
        name="gather",
    )(normed, win, wout)


def total_kernel(
    n, inner_ref, weight_ref, act_ref, gate_ref, sum_ref, zgate_ref, send_buf, recv_buf, own_buf, send, recv, send2, recv2,
):
    req, seq = lax.axis_index("req"), lax.axis_index("seq")
    rows = inner_ref.shape[0] // n
    peers = [(req, (seq + d) % n) for d in range(1, n)]

    def partial(owner):
        block = inner_ref[pl.ds(pl.multiple_of(owner * rows, rows), rows), :]
        return lax.dot_general(
            weight_ref[...], block, (((1,), (1,)), ((), ())), preferred_element_type=jnp.float32
        )

    def gates(first_block, last_block):
        @pl.loop(first_block, last_block)
        def _(i):
            here = pl.ds(pl.multiple_of(i * rows, rows), rows)
            zgate_ref[here, :] = jnp.dot(
                act_ref[here, :], gate_ref[...], preferred_element_type=jnp.float32
            ).astype(jnp.bfloat16)

    greet(peers)
    first = []
    for d in range(1, n):
        send_buf[d - 1] = partial((seq + d) % n).astype(jnp.bfloat16)
        copy = remote(send_buf.at[d - 1], recv_buf.at[d - 1], send.at[d - 1], recv.at[d - 1], peers[d - 1])
        copy.start()
        first.append(copy)
    total = partial(seq)
    gates(0, n // 2)
    for d in range(1, n):
        first[d - 1].wait_recv()
        total = total + recv_buf[d - 1].astype(jnp.float32)
    own_buf[...] = total.astype(jnp.bfloat16)
    second = []
    for d in range(1, n):
        copy = remote(own_buf, sum_ref.at[seq], send2.at[d - 1], recv2.at[d - 1], peers[d - 1])
        copy.start()
        second.append(copy)
    sum_ref[seq] = own_buf[...]
    gates(n // 2, n)
    for copy in second:
        copy.wait()
    for copy in first:
        copy.wait_send()


def total_call(n, inner, weight, act, gate):
    vmem = pl.BlockSpec(memory_space=pltpu.VMEM)
    dma = pltpu.SemaphoreType.DMA
    columns, rows = weight.shape[0], inner.shape[0] // n
    return pl.pallas_call(
        functools.partial(total_kernel, n),
        out_shape=(
            jax.ShapeDtypeStruct((n, columns, rows), jnp.bfloat16),
            jax.ShapeDtypeStruct(inner.shape, jnp.bfloat16),
        ),
        in_specs=[vmem] * 4,
        out_specs=(vmem, vmem),
        scratch_shapes=[
            pltpu.VMEM((n - 1, columns, rows), jnp.bfloat16),
            pltpu.VMEM((n - 1, columns, rows), jnp.bfloat16),
            pltpu.VMEM((columns, rows), jnp.bfloat16),
        ] + [dma((n - 1,))] * 4,
        compiler_params=pltpu.CompilerParams(
            collective_id=1, has_side_effects=True, vmem_limit_bytes=VMEM_LIMIT
        ),
        name="total",
    )(inner, weight, act, gate)


def output_kernel(
    n, m, gated_ref, wout_ref, hidden_ref, state_ref, mixed_ref, slots_ref,
    send_buf, recv_buf, acc_ref, send, recv, state_send, state_recv,
):
    rows, model = hidden_ref.shape
    part = model // STREAMS
    req, seq = lax.axis_index("req"), lax.axis_index("seq")
    place = ring_place(seq, n)
    right = (req, ring_index((place + 1) % n, n))
    left = (req, ring_index((place + n - 1) % n, n))
    peers = [((req + d) % m, seq) for d in range(1, m)]
    greet([left, right] + peers)
    states = []
    for d in range(1, m):
        copy = remote(state_ref, slots_ref.at[req], state_send.at[d - 1], state_recv.at[d - 1], peers[d - 1])
        copy.start()
        states.append(copy)
    slots_ref[req] = state_ref[...]

    def hop(way, step):
        return remote(
            send_buf.at[way, step], recv_buf.at[way, step], send.at[way, step], recv.at[way, step],
            right if way % 2 == 0 else left,
        )

    def product(way, step):
        turn = place + (2 * n - 1 - step if way % 2 == 0 else 1 + step)
        owner = ring_index(turn % n, n)
        block = gated_ref[pl.ds(pl.multiple_of(owner * rows, rows), rows), :]
        acc_ref[way] = jnp.dot(
            block, wout_ref[:, way * part : (way + 1) * part], preferred_element_type=jnp.float32
        )

    for way in range(STREAMS):
        product(way, 0)
        send_buf[way, 0] = acc_ref[way].astype(jnp.bfloat16)
        hop(way, 0).start()

    def middle(step, carry):
        for way in range(STREAMS):
            product(way, step)
        for way in range(STREAMS):
            hop(way, step - 1).wait_recv()
            send_buf[way, step] = (acc_ref[way] + recv_buf[way, step - 1].astype(jnp.float32)).astype(jnp.bfloat16)
            hop(way, step).start()
        return carry

    lax.fori_loop(1, n - 1, middle, 0)
    for way in range(STREAMS):
        product(way, n - 1)
    for way in range(STREAMS):
        hop(way, n - 2).wait_recv()
        columns = slice(way * part, (way + 1) * part)
        branch = acc_ref[way] + recv_buf[way, n - 2].astype(jnp.float32)
        mixed_ref[:, columns] = (hidden_ref[:, columns].astype(jnp.float32) + branch).astype(jnp.bfloat16)
    for step in range(n - 1):
        for way in range(STREAMS):
            hop(way, step).wait_send()
    for copy in states:
        copy.wait()


def output_call(n, m, gated, wout, hidden, state):
    rows, model = hidden.shape
    vmem = pl.BlockSpec(memory_space=pltpu.VMEM)
    dma = pltpu.SemaphoreType.DMA
    return pl.pallas_call(
        functools.partial(output_kernel, n, m),
        out_shape=(
            jax.ShapeDtypeStruct((rows, model), jnp.bfloat16),
            jax.ShapeDtypeStruct((m,) + state.shape, jnp.float32),
        ),
        in_specs=[vmem] * 4,
        out_specs=(vmem, vmem),
        scratch_shapes=[
            pltpu.VMEM((STREAMS, n - 1, rows, model // STREAMS), jnp.bfloat16),
            pltpu.VMEM((STREAMS, n - 1, rows, model // STREAMS), jnp.bfloat16),
            pltpu.VMEM((STREAMS, rows, model // STREAMS), jnp.float32),
            dma((STREAMS, n - 1)), dma((STREAMS, n - 1)), dma((m - 1,)), dma((m - 1,)),
        ],
        compiler_params=pltpu.CompilerParams(
            collective_id=2, has_side_effects=True, vmem_limit_bytes=VMEM_LIMIT
        ),
        name="output",
    )(gated, wout, hidden, state)


def per_device(
    hidden,
    lengths,
    slot_request,
    norm_gain,
    in_weight,
    conv_weight,
    conv_bias,
    xproj_weight,
    dt_weight,
    dt_bias,
    a_log,
    skip_gain,
    out_weight,
):
    seq_count = lax.axis_size("seq")
    seq_index = lax.axis_index("seq")
    req_index = lax.axis_index("req")
    rows = hidden.shape[1]
    span = rows * seq_count
    width = in_weight.shape[2]
    taps_count = conv_weight.shape[0]
    tokens = hidden[0].astype(jnp.float32)
    scale = lax.rsqrt(jnp.mean(tokens * tokens, axis=-1, keepdims=True) + 1e-05)
    normed = (tokens * scale * norm_gain.astype(jnp.float32)).astype(jnp.bfloat16)
    req_count = lax.axis_size("req")
    act, w_in, w_out = gather_call(seq_count, req_count, normed, in_weight, out_weight)
    act = act.reshape(span, -1)
    xin = jnp.dot(act, w_in[0], preferred_element_type=jnp.float32)
    padded = jnp.pad(xin, ((taps_count - 1, 0), (0, 0)))
    taps = conv_weight.astype(jnp.float32)
    convolved = conv_bias.astype(jnp.float32) + jnp.zeros_like(xin)
    for tap in range(taps_count):
        convolved = convolved + taps[tap] * padded[tap : tap + span, :]
    inner = jax.nn.silu(convolved).astype(jnp.bfloat16)
    sums, zgate = total_call(seq_count, inner, xproj_weight.T, act, w_in[1])
    length_here = lax.dynamic_slice_in_dim(lengths, req_index, 1, 0)
    alog = lax.dynamic_slice_in_dim(a_log, seq_index * width, width, 1)
    skip = lax.dynamic_slice_in_dim(skip_gain, seq_index * width, width, 0)[None]
    gated_ch, mine = scan_call(
        length_here, sums, inner, zgate, dt_weight, dt_bias[None], alog, skip
    )
    mixed, slot_all = output_call(seq_count, req_count, gated_ch, w_out, hidden[0], mine)
    picked = (slot_request == req_index).astype(jnp.float32)
    final_state = jnp.sum(picked[:, None, None] * slot_all, axis=0, keepdims=True)
    return (mixed[None], final_state)


def solution(mesh):
    in_specs = (
        P("req", "seq", None),
        P(),
        P(),
        P(),
        P(None, "req", "seq"),
        P(None, "seq"),
        P("seq"),
        P("seq", None),
        P(None, "seq"),
        P("seq"),
        P(),
        P(),
        P("seq", "req"),
    )
    out_specs = (P("req", "seq", None), P("req", None, "seq"))
    return jax.shard_map(
        per_device, mesh=mesh, in_specs=in_specs, out_specs=out_specs, check_vma=False
    )
```
